256 devices in a mesh: pipe: 64 (over y, x, z_lo), tp: 4 (over z_hi, core).
Axes of the slice: x: 4, y: 4, z: 8 (z_hi: 2, z_lo: 4; z = z_hi * 4 + z_lo), core: 2. Of those that a mesh axis runs over, the one named last changes fastest.
Arguments:
- stream_in: bfloat16 [64, 256, 6144], P('pipe', None, 'tp')
- grad_in: bfloat16 [64, 256, 6144], P('pipe', None, 'tp'), may hold values from -6 to 6
- fresh_batch: bfloat16 [256, 6144], P(None, 'tp')
- loss_grad: bfloat16 [256, 6144], P(None, 'tp'), may hold values from -6 to 6
- local_stash: bfloat16 [64, 2, 256, 6144], P('pipe', None, None, 'tp')
- partner_stash: bfloat16 [64, 2, 256, 6144], P('pipe', None, None, 'tp')
- norm_gains: float32 [64, 3, 6144], P('pipe', None, 'tp'), may hold values from 0.25 to 1.75
- stash_plan: int32 [2, 64], replicated, may hold values from 0 to 3, as said below
Outputs:
- fwd_out: bfloat16 [64, 256, 6144], P('pipe', None, 'tp')
- bwd_out: bfloat16 [64, 256, 6144], P('pipe', None, 'tp')
- gain_grad: float32 [64, 3, 6144], P('pipe', None, 'tp')
The draws below stay inside these ranges and needn't reach their ends.
Inputs may be any that keep to these rules, and one draw needn't show every extreme that they name: `stash_plan`: A value k below 2 names the section's own slot k; a value of 2 or more names slot k - 2 of what its mirror partner keeps for it. Sections below 32 always take a stash kept by their partner, the others always one of their own.
All inputs are finite; a program needn't handle non-finite values.
Results may differ from the reference program's by a relative error of at most 0.0097.
Values may be sent and summed in bfloat16 or wider, within the bound.
No kernel may reach another device: no remote copies, remote signals or barrier semaphores. Data moves between devices by JAX's collectives and lax.ppermute only.
A program may use at most 64 MiB of HBM per device.

```python
import jax
import jax.numpy as jnp
from jax import lax

D = 6144
HEAD_DIM = 128
SEQ = 256
SLOTS = 2
TICKS = 2
SECTIONS = 64


def stream_draw(key, lead):
    shape = lead + (SEQ, D)
    return jax.random.normal(key, shape, jnp.float32)


def draw_stream_in(key, part):
    key = jax.random.fold_in(key, 11)
    return stream_draw(key, (SECTIONS,)).astype(jnp.bfloat16)


def draw_fresh_batch(key, part):
    key = jax.random.fold_in(key, 17)
    return stream_draw(key, ()).astype(jnp.bfloat16)


def draw_local_stash(key, part):
    key = jax.random.fold_in(key, 23)
    return stream_draw(key, (SECTIONS, SLOTS)).astype(jnp.bfloat16)


def draw_partner_stash(key, part):
    key = jax.random.fold_in(key, 29)
    return stream_draw(key, (SECTIONS, SLOTS)).astype(jnp.bfloat16)


def draw_stash_plan(key, part):
    key = jax.random.fold_in(key, 41)
    slot_picks = jax.random.randint(key, (TICKS, SECTIONS), 0, SLOTS)
    early = jnp.arange(SECTIONS, dtype=jnp.int32) < SECTIONS // 2
    plan_rows = slot_picks + jnp.where(early, SLOTS, 0)[None, :]
    plan_rows = plan_rows.at[0, 0].set(2 * SLOTS - 1).at[0, SECTIONS - 1].set(0)
    return plan_rows.astype(jnp.int32)


def levels(key, extent, cuts, least, top_value):
    def one(dim, shards_of):
        draws = jax.random.uniform(jax.random.fold_in(jax.random.fold_in(key, 6), dim), (shards_of,), jnp.float32, least / len(cuts), top_value / len(cuts))
        return jnp.repeat(jnp.exp(draws), extent[dim] // shards_of).reshape((-1,) + (1,) * (len(extent) - dim - 1))

    loudness = one(*cuts[0])
    for cut in cuts[1:]:
        loudness = loudness * one(*cut)
    return loudness


def bell_draw(own_key, dims, width, most, cuts=(), kind=jnp.bfloat16):
    result = jax.random.normal(own_key, dims, jnp.float32) * width
    if len(cuts) > 0:
        result = levels(own_key, dims, cuts, -0.22, 0.18) * result
    return jnp.clip(result, min=-most, max=most).astype(kind)


def setup_inputs(seed: int = 0) -> dict:
    seeds = jax.random.split(jax.random.key(seed), 9)
    return {
        "stream_in": draw_stream_in(jax.random.fold_in(seeds[8], 71), 0),
        "grad_in": bell_draw(seeds[1], (SECTIONS, SEQ, D), 1.0, 6.0, ((0, 64), (2, 4))),
        "fresh_batch": draw_fresh_batch(jax.random.fold_in(seeds[8], 71), 0),
        "loss_grad": bell_draw(seeds[3], (SEQ, D), 1.0, 6.0, ((1, 4),)),
        "local_stash": draw_local_stash(jax.random.fold_in(seeds[8], 71), 0),
        "partner_stash": draw_partner_stash(jax.random.fold_in(seeds[8], 71), 0),
        "norm_gains": jnp.clip(1.0 + 0.15 * jax.random.normal(seeds[6], (SECTIONS, 3, D), jnp.float32), 0.25, 1.75),
        "stash_plan": draw_stash_plan(jax.random.fold_in(seeds[8], 71), 0),
    }


EPSILON = 1e-05

def normalize(stream):
    values = stream.astype(jnp.float32)
    center = values - lax.optimization_barrier(jnp.mean(values, axis=-1, keepdims=True))
    spread = lax.optimization_barrier(jnp.mean(center * center, axis=-1, keepdims=True))
    scale_inv = lax.rsqrt(spread + EPSILON)
    return (center * scale_inv, scale_inv)

def projections(normed, gain_rows):
    seq_len = normed.shape[0]
    queries = (normed * gain_rows[0]).astype(jnp.bfloat16).reshape(seq_len, -1, HEAD_DIM)
    key_rows = (normed * gain_rows[1]).astype(jnp.bfloat16).reshape(seq_len, -1, HEAD_DIM)
    value_rows = (normed * gain_rows[2]).astype(jnp.bfloat16).reshape(seq_len, -1, HEAD_DIM)
    return (queries, key_rows, value_rows)

def attention_weights(queries, key_rows):
    seq_len = queries.shape[0]
    scores = jnp.einsum('qhd,khd->hqk', queries.astype(jnp.float32), key_rows.astype(jnp.float32)) * HEAD_DIM ** (-0.5)
    row_ids = lax.broadcasted_iota(jnp.int32, (seq_len, seq_len), 0)
    col_ids = lax.broadcasted_iota(jnp.int32, (seq_len, seq_len), 1)
    scores = jnp.where(col_ids <= row_ids, scores, -1e+30)
    row_top = lax.optimization_barrier(jnp.max(scores, axis=-1, keepdims=True))
    raised = jnp.exp(scores - row_top)
    return raised / lax.optimization_barrier(jnp.sum(raised, axis=-1, keepdims=True))

def forward(stream, gain_rows):
    normed, scale_inv = normalize(stream)
    queries, key_rows, value_rows = projections(normed, gain_rows)
    chances = attention_weights(queries, key_rows)
    weights = chances.astype(jnp.bfloat16)
    context = jnp.einsum('hqk,khd->qhd', weights.astype(jnp.float32), value_rows.astype(jnp.float32))
    return (stream.astype(jnp.float32) + context.reshape(stream.shape[0], -1)).astype(jnp.bfloat16)

def backward(stashed, cotangent, gain_rows):
    seq_len = stashed.shape[0]
    normed, scale_inv = normalize(stashed)
    queries, key_rows, value_rows = projections(normed, gain_rows)
    chances = attention_weights(queries, key_rows)
    weights = chances.astype(jnp.bfloat16)
    cot_heads = cotangent.reshape(seq_len, -1, HEAD_DIM).astype(jnp.float32)
    value_grad = jnp.einsum('hqk,qhd->khd', weights.astype(jnp.float32), cot_heads)
    prob_grad = jnp.einsum('qhd,khd->hqk', cot_heads, value_rows.astype(jnp.float32))
    score_grad = chances * (prob_grad - lax.optimization_barrier(jnp.sum(prob_grad * chances, axis=-1, keepdims=True))) * HEAD_DIM ** (-0.5)
    score_grad = score_grad.astype(jnp.bfloat16).astype(jnp.float32)
    query_grad = jnp.einsum('hqk,khd->qhd', score_grad, key_rows.astype(jnp.float32)).reshape(seq_len, -1)
    key_grad = jnp.einsum('hqk,qhd->khd', score_grad, queries.astype(jnp.float32)).reshape(seq_len, -1)
    value_grad = value_grad.reshape(seq_len, -1)
    normed_grad = query_grad * gain_rows[0] + key_grad * gain_rows[1] + value_grad * gain_rows[2]
    gain_terms = jnp.stack([lax.optimization_barrier(jnp.sum(query_grad * normed, axis=0)), lax.optimization_barrier(jnp.sum(key_grad * normed, axis=0)), lax.optimization_barrier(jnp.sum(value_grad * normed, axis=0))])
    input_grad = scale_inv * (normed_grad - lax.optimization_barrier(jnp.mean(normed_grad, axis=-1, keepdims=True)) - normed * lax.optimization_barrier(jnp.mean(normed_grad * normed, axis=-1, keepdims=True)))
    return ((cotangent.astype(jnp.float32) + input_grad).astype(jnp.bfloat16), gain_terms)

def pick_stash(local_stash, partner_stash, plan_row):
    sections = jnp.arange(plan_row.shape[0], dtype=jnp.int32)
    own_rows = local_stash[sections, jnp.clip(plan_row, 0, SLOTS - 1)]
    kept_rows = partner_stash[::-1][sections, jnp.clip(plan_row - SLOTS, 0, SLOTS - 1)]
    return jnp.where((plan_row < SLOTS)[:, None, None], own_rows, kept_rows)

def reference(stream_in, grad_in, fresh_batch, loss_grad, local_stash, partner_stash, norm_gains, stash_plan):
    stream = stream_in
    cotangent = grad_in
    gain_total = jnp.zeros(norm_gains.shape, jnp.float32)
    for tick_index in range(TICKS):
        if tick_index > 0:
            stream = jnp.concatenate([fresh_batch[None], produced[:-1]], axis=0)
            cotangent = jnp.concatenate([returned[1:], loss_grad[None]], axis=0)
        produced = lax.map(lambda pair: forward(pair[0], pair[1]), (stream, norm_gains))
        stashed = pick_stash(local_stash, partner_stash, stash_plan[tick_index])
        returned, gain_terms = lax.map(lambda group: backward(group[0], group[1], group[2]), (stashed, cotangent, norm_gains))
        gain_total = gain_total + gain_terms
    return (produced, returned, gain_total)
```

```python
import jax
import jax.numpy as jnp
from jax import lax
from jax.experimental import pallas as pl
from jax.experimental.pallas import tpu as pltpu

HEAD_DIM = 128
BLOCK = 128
D = 6144
EPSILON = 1e-05
SCALE = HEAD_DIM ** (-0.5)
HEADS_PER_STEP = 2
VMEM_LIMIT = 40 * 1024 * 1024
F32 = jnp.float32
BF16 = jnp.bfloat16


def dot(a, b, dims):
    return lax.dot_general(a, b, (dims, ((), ())), preferred_element_type=F32)


def to_rows(columns):
    tokens = columns[0].shape[0]
    lane = lax.broadcasted_iota(jnp.int32, (tokens, 128), 1)
    wide = jnp.zeros((tokens, 128), F32)
    for i, column in enumerate(columns):
        wide = jnp.where(lane == i, column, wide)
    return wide.T[:8]


def to_columns(rows):
    filler = jnp.zeros((120, rows.shape[1]), F32)
    return jnp.concatenate([rows, filler], axis=0).T


def moments(values):
    total = jnp.sum(values, axis=-1, keepdims=True)
    center = values - total * (1.0 / values.shape[-1])
    return total, jnp.sum(center * center, axis=-1, keepdims=True)


def causal(s):
    rows, cols = s.shape
    row = lax.broadcasted_iota(jnp.int32, s.shape, 0) + (cols - rows)
    col = lax.broadcasted_iota(jnp.int32, s.shape, 1)
    return jnp.where(col <= row, s, -1e30)


def softmax_rows(q, k):
    s = causal(dot(q, k, ((1,), (1,))) * SCALE)
    raised = jnp.exp(s - jnp.max(s, axis=-1, keepdims=True))
    return raised * (1.0 / jnp.sum(raised, axis=-1, keepdims=True))


def pick_kernel(slots, kept, own, stream, sent, stats):
    columns = []
    picked = kept[0, 0]
    sent[...] = picked
    columns += moments(picked.astype(F32))
    columns += moments(own[0, 0].astype(F32))
    columns += moments(stream[...].astype(F32))
    stats[...] = to_rows(columns)


def pick(slots, kept, own, stream):
    tokens, width = stream.shape
    one = (1, 1, tokens, width)
    return pl.pallas_call(
        pick_kernel,
        grid_spec=pltpu.PrefetchScalarGridSpec(
            num_scalar_prefetch=1,
            grid=(1,),
            in_specs=[
                pl.BlockSpec(one, lambda i, slots: (0, slots[0], 0, 0)),
                pl.BlockSpec(one, lambda i, slots: (0, slots[1], 0, 0)),
                pl.BlockSpec((tokens, width), lambda i, slots: (0, 0)),
            ],
            out_specs=[
                pl.BlockSpec((tokens, width), lambda i, slots: (0, 0)),
                pl.BlockSpec((8, tokens), lambda i, slots: (0, 0)),
            ],
        ),
        out_shape=[
            jax.ShapeDtypeStruct((tokens, width), BF16),
            jax.ShapeDtypeStruct((8, tokens), F32),
        ],
        compiler_params=pltpu.CompilerParams(vmem_limit_bytes=VMEM_LIMIT),
        name="pick",
    )(slots, kept, own, stream)


def head_slice(h):
    return pl.ds(pl.multiple_of(h * HEAD_DIM, HEAD_DIM), HEAD_DIM)


def forward_kernel(flag, a_ref, b_ref, gains, norms, out, stats):
    use_b = flag[0] != 0
    tokens, width = out.shape
    cols = to_columns(norms[...])
    mean = jnp.where(use_b, cols[:, 2:3], cols[:, 0:1])
    rstd = jnp.where(use_b, cols[:, 3:4], cols[:, 1:2])

    def head(h):
        at = head_slice(h)
        x = jnp.where(use_b, b_ref[:, at], a_ref[:, at]).astype(F32)
        n = (x - mean) * rstd
        q = (n * gains[0:1, at]).astype(BF16)
        k = (n * gains[1:2, at]).astype(BF16)
        v = (n * gains[2:3, at]).astype(BF16)
        total = jnp.zeros((tokens, 1), F32)
        for lo in range(0, tokens, BLOCK):
            hi = lo + BLOCK
            w = softmax_rows(q[lo:hi], k[:hi]).astype(BF16)
            context = dot(w, v[:hi], ((1,), (0,)))
            out[lo:hi, at] = (x[lo:hi] + context).astype(BF16)

    def step(i, carry):
        for j in range(HEADS_PER_STEP):
            head(i * HEADS_PER_STEP + j)
        return carry

    lax.fori_loop(0, width // HEAD_DIM // HEADS_PER_STEP, step, 0)
    stats[...] = to_rows(moments(out[...].astype(F32)))


SMEM = pl.BlockSpec(memory_space=pltpu.SMEM)
VMEM = pl.BlockSpec(memory_space=pltpu.VMEM)


def forward(flag, a, b, gains, norms):
    tokens, width = a.shape
    heads = width // HEAD_DIM
    return pl.pallas_call(
        forward_kernel,
        in_specs=[SMEM, VMEM, VMEM, VMEM, VMEM],
        out_specs=[VMEM, VMEM],
        out_shape=[
            jax.ShapeDtypeStruct((tokens, width), BF16),
            jax.ShapeDtypeStruct((8, tokens), F32),
        ],
        compiler_params=pltpu.CompilerParams(vmem_limit_bytes=VMEM_LIMIT),
        cost_estimate=pl.CostEstimate(
            flops=4 * heads * tokens * tokens * HEAD_DIM * 8, bytes_accessed=6 * tokens * width, transcendentals=heads * tokens * tokens
        ),
        name="forward",
    )(flag, a, b, gains, norms)


def backward_kernel(flags, za, zb, ea, eb, gains, norms, before, dn_out, h_out, sums, cross_acc, plain_acc):
    use_zb = flags[0] != 0
    use_eb = flags[1] != 0
    tokens, width = dn_out.shape
    cols = to_columns(norms[...])
    mean = jnp.where(use_zb, cols[:, 2:3], cols[:, 0:1])
    rstd = jnp.where(use_zb, cols[:, 3:4], cols[:, 1:2])
    cross_acc[...] = jnp.zeros_like(cross_acc)
    plain_acc[...] = jnp.zeros_like(plain_acc)

    def head(h):
        at = head_slice(h)
        z = jnp.where(use_zb, zb[:, at], za[:, at]).astype(F32)
        e = jnp.where(use_eb, eb[:, at], ea[:, at])
        n = (z - mean) * rstd
        g0, g1, g2 = gains[0:1, at], gains[1:2, at], gains[2:3, at]
        q = (n * g0).astype(BF16)
        k = (n * g1).astype(BF16)
        v = (n * g2).astype(BF16)
        dq, dk, dv = [], None, None
        for lo in range(0, tokens, BLOCK):
            hi = lo + BLOCK
            p = softmax_rows(q[lo:hi], k[:hi])
            w = p.astype(BF16)
            dp = dot(e[lo:hi], v[:hi], ((1,), (1,)))
            row = jnp.sum(dp * p, axis=-1, keepdims=True)
            ds = (p * (dp - row) * SCALE).astype(BF16)
            dq.append(dot(ds, k[:hi], ((1,), (0,))))
            dv_part = dot(w, e[lo:hi], ((0,), (0,)))
            dk_part = dot(ds, q[lo:hi], ((0,), (0,)))
            if dv is not None:
                dv_part = jnp.concatenate([dv + dv_part[:lo], dv_part[lo:]], axis=0)
                dk_part = jnp.concatenate([dk + dk_part[:lo], dk_part[lo:]], axis=0)
            dv, dk = dv_part, dk_part
        dq = jnp.concatenate(dq, axis=0)
        dn = dq * g0 + dk * g1 + dv * g2
        dn_out[:, at] = dn
        plain_acc[...] += dn
        cross_acc[...] += dn * n
        for i, grad in enumerate((dq, dk, dv)):
            h_out[i : i + 1, at] = before[i : i + 1, at] + jnp.sum(grad * n, axis=0, keepdims=True)

    def step(i, carry):
        for j in range(HEADS_PER_STEP):
            head(i * HEADS_PER_STEP + j)
        return carry

    lax.fori_loop(0, width // HEAD_DIM // HEADS_PER_STEP, step, 0)
    sums[...] = to_rows(
        [jnp.sum(plain_acc[...], axis=-1, keepdims=True), jnp.sum(cross_acc[...], axis=-1, keepdims=True)]
    )


def backward(flags, za, zb, ea, eb, gains, norms, before):
    tokens, width = za.shape
    heads = width // HEAD_DIM
    return pl.pallas_call(
        backward_kernel,
        in_specs=[SMEM] + [VMEM] * 7,
        out_specs=[VMEM] * 3,
        out_shape=[
            jax.ShapeDtypeStruct((tokens, width), F32),
            jax.ShapeDtypeStruct((3, width), F32),
            jax.ShapeDtypeStruct((8, tokens), F32),
        ],
        scratch_shapes=[pltpu.VMEM((tokens, HEAD_DIM), F32), pltpu.VMEM((tokens, HEAD_DIM), F32)],
        compiler_params=pltpu.CompilerParams(vmem_limit_bytes=VMEM_LIMIT),
        cost_estimate=pl.CostEstimate(
            flops=14 * heads * tokens * tokens * HEAD_DIM * 8, bytes_accessed=10 * tokens * width, transcendentals=heads * tokens * tokens
        ),
        name="backward",
    )(flags, za, zb, ea, eb, gains, norms, before)


def finish_kernel(flags, za, zb, ea, eb, norms, dn, sums, out):
    use_zb = flags[0] != 0
    use_eb = flags[1] != 0
    cols = to_columns(norms[...])
    mean = jnp.where(use_zb, cols[:, 2:3], cols[:, 0:1])
    rstd = jnp.where(use_zb, cols[:, 3:4], cols[:, 1:2])
    means = to_columns(sums[...])
    plain, cross = means[:, 0:1] * (1.0 / D), means[:, 1:2] * (1.0 / D)

    def step(h, carry):
        at = head_slice(h)
        z = jnp.where(use_zb, zb[:, at], za[:, at]).astype(F32)
        e = jnp.where(use_eb, eb[:, at], ea[:, at]).astype(F32)
        n = (z - mean) * rstd
        out[:, at] = (e + rstd * (dn[:, at] - plain - n * cross)).astype(BF16)
        return carry

    lax.fori_loop(0, out.shape[1] // HEAD_DIM, step, 0)


def finish(flags, za, zb, ea, eb, norms, dn, sums):
    tokens, width = za.shape
    return pl.pallas_call(
        finish_kernel,
        in_specs=[SMEM] + [VMEM] * 7,
        out_specs=VMEM,
        out_shape=jax.ShapeDtypeStruct((tokens, width), BF16),
        compiler_params=pltpu.CompilerParams(vmem_limit_bytes=VMEM_LIMIT),
        name="finish",
    )(flags, za, zb, ea, eb, norms, dn, sums)


def over_tp(rows, combine):
    for mask in (1, 2):
        rows = combine(rows, lax.ppermute(rows, "tp", [(i, i ^ mask) for i in range(4)]))
    return rows


def joined(width):
    count = [width]

    def combine(mine, other):
        a, b = mine.reshape(-1, 2, mine.shape[-1]), other.reshape(-1, 2, mine.shape[-1])
        apart = (a[:, 0] - b[:, 0]) / count[0]
        squares = a[:, 1] + b[:, 1] + apart * apart * (0.5 * count[0])
        count[0] *= 2
        return jnp.stack([a[:, 0] + b[:, 0], squares], axis=1).reshape(mine.shape)

    return combine


def norm_rows(rows):
    pairs = rows.reshape(-1, 2, rows.shape[-1]) / D
    return jnp.stack([pairs[:, 0], lax.rsqrt(pairs[:, 1] + EPSILON)], axis=1).reshape(rows.shape)


def per_device(
    stream_in, grad_in, fresh_batch, loss_grad, local_stash, partner_stash, norm_gains, stash_plan
):
    sections = lax.axis_size("pipe")
    half = sections // 2
    section = lax.axis_index("pipe")
    slots = local_stash.shape[1]
    gains = norm_gains[0]
    stream, cotangent = stream_in[0], grad_in[0]
    width = stream.shape[1]

    to_next = [(i, i + 1) for i in range(sections - 1)]
    to_last = [(i + 1, i) for i in range(sections - 1)]
    mirrored = [(sections - 1 - s, s) for s in range(half)]

    kept_at = jnp.clip(stash_plan[:, sections - 1 - section] - slots, 0, slots - 1)
    own_at = jnp.clip(stash_plan[:, section], 0, slots - 1)
    early = (section < half).astype(jnp.int32)
    first = (section == 0).astype(jnp.int32)
    last = (section == sections - 1).astype(jnp.int32)

    sent0, rows0 = pick(jnp.stack([kept_at[0], own_at[0]]), partner_stash, local_stash, stream)
    z0 = lax.ppermute(sent0, "pipe", mirrored)
    sent1, rows1 = pick(jnp.stack([kept_at[1], own_at[1]]), partner_stash, local_stash, fresh_batch)
    z1 = lax.ppermute(sent1, "pipe", mirrored)
    own0 = lax.dynamic_index_in_dim(local_stash[0], own_at[0], 0, keepdims=False)
    own1 = lax.dynamic_index_in_dim(local_stash[0], own_at[1], 0, keepdims=False)

    norms = norm_rows(over_tp(jnp.concatenate([rows0[:6], rows1[:6]], axis=0), joined(width)))
    got = lax.ppermute(jnp.concatenate([norms[0:2], norms[6:8]], axis=0), "pipe", mirrored)
    fill = jnp.zeros((4, norms.shape[1]), F32)
    norms_z0 = jnp.concatenate([norms[2:4], got[0:2], fill], axis=0)
    norms_z1 = jnp.concatenate([norms[8:10], got[2:4], fill], axis=0)

    produced, out_rows = forward(jnp.zeros((1,), jnp.int32), stream, stream, gains, jnp.concatenate([norms[4:6], norms[4:6], fill]))
    arrived = lax.ppermute(produced, "pipe", to_next)
    flags0 = jnp.stack([early, jnp.zeros_like(early)])
    grad, gain_total, sums = backward(
        flags0, own0, z0, cotangent, cotangent, gains, norms_z0, jnp.zeros((3, width), F32)
    )
    out_norms = norm_rows(over_tp(out_rows[:2], joined(width)))
    out_norms = lax.ppermute(out_norms, "pipe", to_next)
    sums = over_tp(sums, lambda a, b: a + b)
    returned = finish(flags0, own0, z0, cotangent, cotangent, norms_z0, grad, sums)
    came_back = lax.ppermute(returned, "pipe", to_last)

    fwd_out, _ = forward(
        jnp.stack([first]), arrived, fresh_batch, gains, jnp.concatenate([out_norms, norms[10:12], fill])
    )
    flags1 = jnp.stack([early, last])
    grad, gain_total, sums = backward(flags1, own1, z1, came_back, loss_grad, gains, norms_z1, gain_total)
    sums = over_tp(sums, lambda a, b: a + b)
    bwd_out = finish(flags1, own1, z1, came_back, loss_grad, norms_z1, grad, sums)
    return (fwd_out[None], bwd_out[None], gain_total[None])


def solution(mesh):
    from jax.sharding import PartitionSpec as P

    placed = (
        P("pipe", None, "tp"),
        P("pipe", None, "tp"),
        P(None, "tp"),
        P(None, "tp"),
        P("pipe", None, None, "tp"),
        P("pipe", None, None, "tp"),
        P("pipe", None, "tp"),
        P(),
    )
    return jax.shard_map(
        per_device,
        mesh=mesh,
        in_specs=placed,
        out_specs=(P("pipe", None, "tp"), P("pipe", None, "tp"), P("pipe", None, "tp")),
        check_vma=False,
    )
```

```python
import jax
import jax.numpy as jnp
from jax import lax
from jax.experimental import pallas as pl
from jax.experimental.pallas import tpu as pltpu
from jax.sharding import PartitionSpec as P

HEAD_DIM = 128
BLOCK = 128
D = 6144
PARTS = 4
EPSILON = 1e-05
SCALE = HEAD_DIM ** (-0.5)
EXP2_SCALE = SCALE * 1.4426950408889634
HEADS_PER_STEP = 6
DIRECT_HEADS = 4
F32 = jnp.float32
BF16 = jnp.bfloat16
SMEM = pl.BlockSpec(memory_space=pltpu.SMEM)
VMEM = pl.BlockSpec(memory_space=pltpu.VMEM)
HBM = pl.BlockSpec(memory_space=pltpu.HBM)
PARAMS = pltpu.CompilerParams(vmem_limit_bytes=16 * 1024 * 1024)
ALL_VMEM = pltpu.CompilerParams(vmem_limit_bytes=56 * 1024 * 1024)


def dot(a, b, dims):
    return lax.dot_general(a, b, (dims, ((), ())), preferred_element_type=F32)


OWN_STASH0, OWN_STASH1, KEPT_STASH0, KEPT_STASH1, STREAM, FRESH = range(6)


def to_rows(columns):
    tokens = next(c for c in columns if c is not None).shape[0]
    lane = lax.broadcasted_iota(jnp.int32, (tokens, 128), 1)
    wide = jnp.zeros((tokens, 128), F32)
    for i, column in enumerate(columns):
        if column is not None:
            wide = jnp.where(lane == i, column, wide)
    return wide.T[: max(8, len(columns))]


def statistics_rows(found):
    columns = [None] * 16
    for place, (total, squares) in found.items():
        columns[place], columns[place + 8] = total, squares
    return to_rows(columns)


def spread(row):
    return jnp.broadcast_to(row, (HEAD_DIM, row.shape[1])).T


def moments(values):
    total = jnp.sum(values, axis=-1, keepdims=True)
    center = values - total * (1.0 / values.shape[-1])
    return total, jnp.sum(center * center, axis=-1, keepdims=True)


def joined_pair(sums, squares, other_sums, other_squares, count):
    apart = sums - other_sums
    return sums + other_sums, squares + other_squares + apart * apart * (0.5 / count)


def join_statistics(a, b, count):
    return jnp.concatenate(joined_pair(a[0:8], a[8:16], b[0:8], b[8:16], count), axis=0)


def join_gradients(a, b, count):
    total, squares = joined_pair(a[2:3], a[3:4], b[2:3], b[3:4], count)
    return jnp.concatenate([a[0:2] + b[0:2], total, squares, a[4:8]], axis=0)


def normalizer(total, squares):
    return total * (1.0 / D), lax.rsqrt(squares * (1.0 / D) + EPSILON)


def half_count(width):
    return width * (PARTS // 2)


def statistics_norm(mine, other, which, width):
    both = join_statistics(mine[...], other[...], half_count(width))
    return normalizer(both[which : which + 1], both[which + 8 : which + 9])


def gradients_norm(mine, other, width):
    both = join_gradients(mine[...], other[...], half_count(width))
    return normalizer(both[2:3], both[3:4])


def slot_of(plan, tick, section, first):
    return jnp.clip(plan[tick, section] - first, 0, 1)


def pick_kernel(plan, kept, own, stream, fresh, sent0, direct, around, own0, own1, rows, buffers, sems):
    section, sections = lax.axis_index("pipe"), plan.shape[1]
    cut = direct.shape[1]
    partner = sections - 1 - section
    copies = [
        pltpu.make_async_copy(kept.at[0, slot_of(plan, 0, partner, 2)], sent0, sems.at[0]),
        pltpu.make_async_copy(kept.at[0, slot_of(plan, 1, partner, 2)], buffers.at[0], sems.at[1]),
        pltpu.make_async_copy(own.at[0, slot_of(plan, 0, section, 0)], own0, sems.at[2]),
        pltpu.make_async_copy(own.at[0, slot_of(plan, 1, section, 0)], own1, sems.at[3]),
        pltpu.make_async_copy(stream.at[0], buffers.at[1], sems.at[4]),
        pltpu.make_async_copy(fresh, buffers.at[2], sems.at[5]),
    ]
    refs = [sent0, buffers.at[0], own0, own1, buffers.at[1], buffers.at[2]]
    places = (KEPT_STASH0, KEPT_STASH1, OWN_STASH0, OWN_STASH1, STREAM, FRESH)
    for copy in copies:
        copy.start()
    found = {}
    for place, copy, ref in zip(places, copies, refs):
        copy.wait()
        found[place] = moments(ref[...].astype(F32))
    rows[...] = statistics_rows(found)
    direct[...] = buffers[0, :, :cut]
    around[...] = buffers[0, :, cut:]


def pick(plan, kept, own, stream, fresh):
    tokens, width = fresh.shape
    cut = DIRECT_HEADS * HEAD_DIM
    whole = jax.ShapeDtypeStruct((tokens, width), BF16)
    return pl.pallas_call(
        pick_kernel,
        in_specs=[SMEM, HBM, HBM, HBM, HBM],
        out_specs=[VMEM] * 6,
        out_shape=[
            whole,
            jax.ShapeDtypeStruct((tokens, cut), BF16),
            jax.ShapeDtypeStruct((tokens, width - cut), BF16),
            whole,
            whole,
            jax.ShapeDtypeStruct((16, tokens), F32),
        ],
        scratch_shapes=[pltpu.VMEM((3, tokens, width), BF16), pltpu.SemaphoreType.DMA((6,))],
        compiler_params=ALL_VMEM,
        name="pick",
    )(plan, kept, own, stream, fresh)


def head_slice(h):
    return pl.ds(pl.multiple_of(h * HEAD_DIM, HEAD_DIM), HEAD_DIM)


def each_head(heads, body):
    def step(i, carry):
        for j in range(HEADS_PER_STEP):
            body(i * HEADS_PER_STEP + j)
        return carry

    lax.fori_loop(0, heads // HEADS_PER_STEP, step, 0)


def causal(s):
    key = lax.broadcasted_iota(jnp.int32, s.shape, 0)
    query = lax.broadcasted_iota(jnp.int32, s.shape, 1)
    return jnp.where(key <= query, s, -1e30)


def softmax_block(s, lo):
    s = s * EXP2_SCALE
    s = jnp.concatenate([s[:lo], causal(s[lo:])], axis=0) if lo else causal(s)
    raised = jnp.exp2(s - jnp.max(s, axis=0, keepdims=True))
    return raised * (1.0 / jnp.sum(raised, axis=0, keepdims=True))


def padded(block, tokens):
    missing = tokens - block.shape[0]
    return jnp.concatenate([block, jnp.zeros((missing, block.shape[1]), block.dtype)], axis=0) if missing else block


def forward_body(pick, gains, norm, out, mean, rstd):
    tokens, width = out.shape
    mean[...] = spread(norm[0])
    rstd[...] = spread(norm[1])

    def head(h):
        at = head_slice(h)
        x = pick(at).astype(F32)
        n = (x - mean[...]) * rstd[...]
        q = (n * gains[0:1, at]).astype(BF16)
        k = (n * gains[1:2, at]).astype(BF16)
        v = (n * gains[2:3, at]).astype(BF16)
        scores = dot(k, q, ((1,), (1,)))
        w = []
        for lo in range(0, tokens, BLOCK):
            hi = lo + BLOCK
            w.append(padded(softmax_block(scores[:hi, lo:hi], lo).astype(BF16), tokens))
        out[:, at] = (x + dot(jnp.concatenate(w, axis=1), v, ((0,), (0,)))).astype(BF16)

    each_head(width // HEAD_DIM, head)


def forward0_kernel(stream, gains, mine, other, out, rows, mean, rstd):
    norm = statistics_norm(mine, other, STREAM, out.shape[1])
    forward_body(lambda at: stream[:, at], gains, norm, out, mean, rstd)
    total, squares = moments(out[...].astype(F32))
    rows[...] = to_rows([None, None, total, squares])


def forward1_kernel(arrived, fresh, gains, late_mine, late_other, mine, other, out, mean, rstd):
    first = lax.axis_index("pipe") == 0
    width = out.shape[1]
    norm = [
        jnp.where(first, a, b)
        for a, b in zip(statistics_norm(mine, other, FRESH, width), gradients_norm(late_mine, late_other, width))
    ]
    forward_body(lambda at: jnp.where(first, fresh[:, at], arrived[:, at]), gains, norm, out, mean, rstd)


def local_call(kernel, out_shape, scratch, operands, name):
    return pl.pallas_call(
        kernel,
        in_specs=[VMEM] * len(operands),
        out_specs=[VMEM] * len(out_shape),
        out_shape=out_shape,
        scratch_shapes=scratch,
        compiler_params=PARAMS,
        name=name,
    )(*operands)


def forward(kernel, name, with_rows, *operands):
    tokens, width = operands[0].shape
    out_shape = [jax.ShapeDtypeStruct((tokens, width), BF16)]
    if with_rows:
        out_shape.append(jax.ShapeDtypeStruct((8, tokens), F32))
    return local_call(kernel, out_shape, [pltpu.VMEM((tokens, HEAD_DIM), F32)] * 2, operands, name)


def backward_body(pick, pick_gains, norm, before, dn_out, h_out, sums, mean, rstd, plain, cross):
    tokens, width = dn_out.shape
    mean[...] = spread(norm[0])
    rstd[...] = spread(norm[1])
    plain[...] = jnp.zeros_like(plain)
    cross[...] = jnp.zeros_like(cross)

    def head(h):
        at = head_slice(h)
        z, e = pick(h, at)
        n = (z.astype(F32) - mean[...]) * rstd[...]
        g = pick_gains(at)
        g0, g1, g2 = g[0:1], g[1:2], g[2:3]
        q = (n * g0).astype(BF16)
        k = (n * g1).astype(BF16)
        v = (n * g2).astype(BF16)
        scores = dot(k, q, ((1,), (1,)))
        dp = dot(v, e, ((1,), (1,)))
        w, ds = [], []
        for lo in range(0, tokens, BLOCK):
            hi = lo + BLOCK
            p = softmax_block(scores[:hi, lo:hi], lo)
            t = p * dp[:hi, lo:hi]
            w.append(padded(p.astype(BF16), tokens))
            ds.append(padded((t - p * jnp.sum(t, axis=0, keepdims=True)).astype(BF16), tokens))
        w, ds = jnp.concatenate(w, axis=1), jnp.concatenate(ds, axis=1)
        dv = dot(w, e, ((1,), (0,)))
        dk = dot(ds, q, ((1,), (0,)))
        dq = dot(ds, k, ((0,), (0,)))
        dn = dq * (g0 * SCALE) + dk * (g1 * SCALE) + dv * g2
        dn_out[:, at] = dn
        plain[...] += dn
        cross[...] += dn * n
        parts = [jnp.sum(grad * n, axis=0, keepdims=True) for grad in (dq, dk, dv)]
        total = jnp.concatenate([parts[0] * SCALE, parts[1] * SCALE, parts[2]], axis=0)
        h_out[0:3, at] = total if before is None else total + before(at)

    each_head(width // HEAD_DIM, head)
    sums[...] = to_rows([jnp.sum(plain[...], axis=-1, keepdims=True), jnp.sum(cross[...], axis=-1, keepdims=True)])


def finish_body(pick, norm, mine, other, dn, out, mean, rstd, plain, cross):
    means = (mine[0:2] + other[0:2]) * (1.0 / D)
    mean[...] = spread(norm[0])
    rstd[...] = spread(norm[1])
    plain[...] = spread(means[0:1])
    cross[...] = spread(means[1:2])

    def head(h):
        at = head_slice(h)
        z, e = pick(h, at)
        n = (z.astype(F32) - mean[...]) * rstd[...]
        out[:, at] = (e.astype(F32) + rstd[...] * (dn[:, at] - plain[...] - n * cross[...])).astype(BF16)

    each_head(out.shape[1] // HEAD_DIM, head)


def is_early():
    return lax.axis_index("pipe") < lax.axis_size("pipe") // 2


def pick_tick1(own_z, direct_z, around_z, own_e, got_e, loss_e):
    section, sections = lax.axis_index("pipe"), lax.axis_size("pipe")
    early = section < sections // 2
    here = section < sections // 2 - 1
    last = section == sections - 1

    def pick(h, at):
        first = jnp.minimum(h, DIRECT_HEADS - 1)
        second = jnp.maximum(h - DIRECT_HEADS, 0)
        got = jnp.where(h < DIRECT_HEADS, direct_z[:, head_slice(first)], around_z[:, head_slice(second)])
        e = jnp.where(last, loss_e[:, at], jnp.where(here, own_e[:, at], got_e[:, at]))
        return jnp.where(early, got, own_z[:, at]), e

    return pick


def late_backward0_kernel(z, e, gains, mine, other, *rest):
    @pl.when(jnp.logical_not(is_early()))
    def _():
        norm = statistics_norm(mine, other, OWN_STASH0, rest[0].shape[1])
        backward_body(lambda h, at: (z[:, at], e[:, at]), lambda at: gains[:, at], norm, None, *rest)


def early_backward0_kernel(z, e, gains, got_stats, dn, h_out, *rest):
    @pl.when(is_early())
    def _():
        tokens, width = dn.shape
        norm = normalizer(got_stats[0:1], got_stats[2:3])
        backward_body(lambda h, at: (z[:, at], e[:, at]), lambda at: gains[:, at], norm, None, dn, h_out, *rest)
        h_out[3:4, :] = jnp.zeros((1, width), F32)
        h_out[3:4, 0:tokens] = got_stats[1:2]
        h_out[3:4, tokens : 2 * tokens] = got_stats[3:4]


def late_finish0_kernel(z, e, stats_mine, stats_other, mine, other, dn, out, *rest):
    @pl.when(jnp.logical_not(is_early()))
    def _():
        norm = statistics_norm(stats_mine, stats_other, OWN_STASH0, out.shape[1])
        finish_body(lambda h, at: (z[:, at], e[:, at]), norm, mine, other, dn, out, *rest)


def early_finish0_kernel(z, e, got_stats, mine, other, dn, out, *rest):
    @pl.when(is_early())
    def _():
        norm = normalizer(got_stats[0:1], got_stats[2:3])
        finish_body(lambda h, at: (z[:, at], e[:, at]), norm, mine, other, dn, out, *rest)


def tick1_norm(mine, other, got_part, width):
    early, tokens = is_early(), mine.shape[1]
    sent = normalizer(got_part[3:4, 0:tokens], got_part[3:4, tokens : 2 * tokens])
    return [jnp.where(early, a, b) for a, b in zip(sent, statistics_norm(mine, other, OWN_STASH1, width))]


def backward1_kernel(oz, dz, az, oe, ge, le, gains, part, got_part, mine, other, dn, h_out, *rest):
    early = is_early()
    backward_body(
        pick_tick1(oz, dz, az, oe, ge, le),
        lambda at: gains[:, at],
        tick1_norm(mine, other, got_part, dn.shape[1]),
        lambda at: jnp.where(early, got_part[0:3, at], part[0:3, at]),
        dn,
        h_out,
        *rest,
    )


def finish1_kernel(oz, dz, az, oe, ge, le, stats_mine, stats_other, got_part, mine, other, dn, out, *rest):
    norm = tick1_norm(stats_mine, stats_other, got_part, out.shape[1])
    finish_body(pick_tick1(oz, dz, az, oe, ge, le), norm, mine, other, dn, out, *rest)


def backward(kernel, name, gain_rows, *operands):
    tokens, width = operands[0].shape
    out_shape = [
        jax.ShapeDtypeStruct((tokens, width), F32),
        jax.ShapeDtypeStruct((gain_rows, width), F32),
        jax.ShapeDtypeStruct((8, tokens), F32),
    ]
    return local_call(kernel, out_shape, [pltpu.VMEM((tokens, HEAD_DIM), F32)] * 4, operands, name)


def finish(kernel, name, *operands):
    tokens, width = operands[0].shape
    out_shape = [jax.ShapeDtypeStruct((tokens, width), BF16)]
    return local_call(kernel, out_shape, [pltpu.VMEM((tokens, HEAD_DIM), F32)] * 4, operands, name)[0]


def routes(sections):
    half, last = sections // 2, sections - 1
    to_next = [(s, s + 1) for s in range(last)]
    late_back = [(s, s - 1) for s in range(half, sections)]
    early_back = [(s, (s - 1) % half) for s in range(half)]
    early_on = [(s, (s + 1) % half) for s in range(half)]
    stash_ahead = [(last - s, (s - 1) % half) for s in range(half)]
    mirrored = [(last - s, s) for s in range(half)]
    across = [(last - s, s ^ 3) for s in range(half)]
    along = [(s ^ 3, s) for s in range(half)]
    return to_next, late_back, early_back, early_on, stash_ahead, mirrored, across, along


def over_tp(value, mask, sections=None):
    if sections is None:
        return lax.ppermute(value, "tp", [(i, i ^ mask) for i in range(PARTS)])
    pairs = [(s * PARTS + i, s * PARTS + (i ^ mask)) for s in sections for i in range(PARTS)]
    return lax.ppermute(value, ("pipe", "tp"), pairs)


def per_device(
    stream_in, grad_in, fresh_batch, loss_grad, local_stash, partner_stash, norm_gains, stash_plan
):
    gains = norm_gains[0]
    cotangent = grad_in[0]
    width = fresh_batch.shape[1]
    to_next, late_back, early_back, early_on, stash_ahead, mirrored, across, along = routes(lax.axis_size("pipe"))

    def moved(value, pairs):
        return lax.ppermute(value, "pipe", pairs)

    def after(value, *others):
        return lax.optimization_barrier((value,) + others)[0]

    half = lax.axis_size("pipe") // 2
    low, high = range(half), range(half, 2 * half)
    sent0, direct, around, own_z0, own_z1, rows = pick(
        stash_plan, partner_stash, local_stash, stream_in, fresh_batch
    )
    got_z0 = moved(sent0, stash_ahead)
    got_e0 = moved(cotangent, early_back)
    got_gains = moved(gains, early_back)
    stats_mine = join_statistics(rows, over_tp(rows, 1), width)
    late_other = over_tp(stats_mine, 2, high)
    late_stats = (stats_mine, late_other)
    both = join_statistics(*late_stats, half_count(width))
    kept = [both[place : place + 1] for place in (KEPT_STASH0, KEPT_STASH1, KEPT_STASH0 + 8, KEPT_STASH1 + 8)]
    got_stats = moved(jnp.concatenate(kept), stash_ahead)
    stats = (stats_mine, late_other + over_tp(stats_mine, 2, low))

    late_tick0 = (own_z0, cotangent)
    grad, late_part, sums = backward(late_backward0_kernel, "late_backward0", 3, *late_tick0, gains, *late_stats)
    sums_mine = sums + over_tp(sums, 1, high)
    sums_other = over_tp(sums_mine, 2, high)
    produced, out_rows = forward(forward0_kernel, "forward0", True, after(stream_in[0], sums_mine), gains, *stats)
    grad = after(grad, produced)
    late_returned = finish(
        late_finish0_kernel, "late_finish0", *late_tick0, *late_stats, sums_mine, sums_other, grad
    )
    came_back = moved(late_returned, late_back)
    got_out_rows = moved(out_rows, to_next)
    around = moved(after(around, got_stats, late_returned), across)
    got_z1a = moved(after(direct, got_stats, late_returned), mirrored)

    early_tick0 = (got_z0, got_e0)
    grad, early_part, sums = backward(
        early_backward0_kernel, "early_backward0", 4, *early_tick0, got_gains, after(got_stats, late_returned)
    )
    gain_back = moved(early_part, early_on)
    sums_mine = sums + over_tp(sums, 1, low)
    sums_other = over_tp(sums_mine, 2, low)
    grad, around = lax.optimization_barrier((grad, around, gain_back, got_out_rows))[:2]
    early_returned = finish(
        early_finish0_kernel, "early_finish0", *early_tick0, got_stats, sums_mine, sums_other, grad
    )
    got_z1b = moved(around, along)
    arrived = moved(after(produced, early_returned), to_next)

    tick1 = (own_z1, got_z1a, got_z1b, early_returned, came_back, loss_grad)
    grad, gain_total, sums = backward(
        backward1_kernel, "backward1", 3, *tick1, gains, late_part, gain_back, *late_stats
    )
    rows = sums + got_out_rows
    sums_mine = join_gradients(rows, over_tp(rows, 1), width)
    sums1 = (sums_mine, over_tp(sums_mine, 2))
    fwd_out = forward(forward1_kernel, "forward1", False, arrived, fresh_batch, gains, *sums1, *stats)[0]
    bwd_out = finish(finish1_kernel, "finish1", *tick1, *late_stats, gain_back, *sums1, grad)
    return (fwd_out[None], bwd_out[None], gain_total[None])


def solution(mesh):
    placed = (
        P("pipe", None, "tp"),
        P("pipe", None, "tp"),
        P(None, "tp"),
        P(None, "tp"),
        P("pipe", None, None, "tp"),
        P("pipe", None, None, "tp"),
        P("pipe", None, "tp"),
        P(),
    )
    return jax.shard_map(
        per_device,
        mesh=mesh,
        in_specs=placed,
        out_specs=(P("pipe", None, "tp"), P("pipe", None, "tp"), P("pipe", None, "tp")),
        check_vma=False,
    )
```

```python
import jax
import jax.numpy as jnp
from jax import lax
from jax.experimental import pallas as pl
from jax.experimental.pallas import tpu as pltpu
from jax.sharding import PartitionSpec as P

HEAD_DIM = 128
BLOCK = 128
D = 6144
PARTS = 4
EPSILON = 1e-05
SCALE = HEAD_DIM ** (-0.5)
EXP2_SCALE = SCALE * 1.4426950408889634
HEADS_PER_STEP = 6
DIRECT_HEADS = 4
F32 = jnp.float32
BF16 = jnp.bfloat16
SMEM = pl.BlockSpec(memory_space=pltpu.SMEM)
VMEM = pl.BlockSpec(memory_space=pltpu.VMEM)
HBM = pl.BlockSpec(memory_space=pltpu.HBM)
PARAMS = pltpu.CompilerParams(vmem_limit_bytes=16 * 1024 * 1024)
ALL_VMEM = pltpu.CompilerParams(vmem_limit_bytes=56 * 1024 * 1024)


def dot(a, b, dims):
    return lax.dot_general(a, b, (dims, ((), ())), preferred_element_type=F32)


OWN_STASH0, OWN_STASH1, KEPT_STASH0, KEPT_STASH1, STREAM, FRESH = range(6)


def to_rows(columns):
    tokens = next(c for c in columns if c is not None).shape[0]
    lane = lax.broadcasted_iota(jnp.int32, (tokens, 128), 1)
    wide = jnp.zeros((tokens, 128), F32)
    for i, column in enumerate(columns):
        if column is not None:
            wide = jnp.where(lane == i, column, wide)
    return wide.T[: max(8, len(columns))]


def statistics_rows(found):
    columns = [None] * 16
    for place, (total, squares) in found.items():
        columns[place], columns[place + 8] = total, squares
    return to_rows(columns)


def spread(row):
    return jnp.broadcast_to(row, (HEAD_DIM, row.shape[1])).T


def moments(values):
    total = jnp.sum(values, axis=-1, keepdims=True)
    center = values - total * (1.0 / values.shape[-1])
    return total, jnp.sum(center * center, axis=-1, keepdims=True)


def joined_pair(sums, squares, other_sums, other_squares, count):
    apart = sums - other_sums
    return sums + other_sums, squares + other_squares + apart * apart * (0.5 / count)


def join_statistics(a, b, count):
    return jnp.concatenate(joined_pair(a[0:8], a[8:16], b[0:8], b[8:16], count), axis=0)


def join_gradients(a, b, count):
    total, squares = joined_pair(a[2:3], a[3:4], b[2:3], b[3:4], count)
    return jnp.concatenate([a[0:2] + b[0:2], total, squares, a[4:8]], axis=0)


def normalizer(total, squares):
    return total * (1.0 / D), lax.rsqrt(squares * (1.0 / D) + EPSILON)


def half_count(width):
    return width * (PARTS // 2)


def statistics_norm(mine, other, which, width):
    both = join_statistics(mine[...], other[...], half_count(width))
    return normalizer(both[which : which + 1], both[which + 8 : which + 9])


def gradients_norm(mine, other, width):
    both = join_gradients(mine[...], other[...], half_count(width))
    return normalizer(both[2:3], both[3:4])


def slot_of(plan, tick, section, first):
    return jnp.clip(plan[tick, section] - first, 0, 1)


def pick_kernel(plan, kept, own, stream, fresh, sent0, direct, around, own0, own1, rows, blocks, load_sems, store_sems):
    section, sections = lax.axis_index("pipe"), plan.shape[1]
    cut = direct.shape[1]
    partner = sections - 1 - section
    sources = [
        (KEPT_STASH1, kept.at[0, slot_of(plan, 1, partner, 2)]),
        (KEPT_STASH0, kept.at[0, slot_of(plan, 0, partner, 2)]),
        (OWN_STASH0, own.at[0, slot_of(plan, 0, section, 0)]),
        (OWN_STASH1, own.at[0, slot_of(plan, 1, section, 0)]),
        (STREAM, stream.at[0]),
        (FRESH, fresh),
    ]
    loads = [pltpu.make_async_copy(source, blocks.at[i], load_sems.at[i]) for i, (_, source) in enumerate(sources)]
    stores = [
        (0, pltpu.make_async_copy(blocks.at[0, :, pl.ds(0, cut)], direct, store_sems.at[0])),
        (0, pltpu.make_async_copy(blocks.at[0, :, pl.ds(cut, around.shape[1])], around, store_sems.at[1])),
        (1, pltpu.make_async_copy(blocks.at[1], sent0, store_sems.at[2])),
        (2, pltpu.make_async_copy(blocks.at[2], own0, store_sems.at[3])),
        (3, pltpu.make_async_copy(blocks.at[3], own1, store_sems.at[4])),
    ]
    for load in loads:
        load.start()
    found = {}
    for i, (place, _) in enumerate(sources):
        loads[i].wait()
        for block, store in stores:
            if block == i:
                store.start()
        found[place] = moments(blocks[i].astype(F32))
    rows[...] = statistics_rows(found)
    for _, store in stores:
        store.wait()


def pick(plan, kept, own, stream, fresh):
    tokens, width = fresh.shape
    cut = DIRECT_HEADS * HEAD_DIM
    whole = jax.ShapeDtypeStruct((tokens, width), BF16)
    return pl.pallas_call(
        pick_kernel,
        in_specs=[SMEM, HBM, HBM, HBM, HBM],
        out_specs=[HBM] * 5 + [VMEM],
        out_shape=[
            whole,
            jax.ShapeDtypeStruct((tokens, cut), BF16),
            jax.ShapeDtypeStruct((tokens, width - cut), BF16),
            whole,
            whole,
            jax.ShapeDtypeStruct((16, tokens), F32),
        ],
        scratch_shapes=[
            pltpu.VMEM((6, tokens, width), BF16),
            pltpu.SemaphoreType.DMA((6,)),
            pltpu.SemaphoreType.DMA((5,)),
        ],
        compiler_params=ALL_VMEM,
        name="pick",
    )(plan, kept, own, stream, fresh)


def head_slice(h):
    return pl.ds(pl.multiple_of(h * HEAD_DIM, HEAD_DIM), HEAD_DIM)


def each_head(heads, body):
    def step(i, carry):
        for j in range(HEADS_PER_STEP):
            body(i * HEADS_PER_STEP + j)
        return carry

    lax.fori_loop(0, heads // HEADS_PER_STEP, step, 0)


def causal(s):
    key = lax.broadcasted_iota(jnp.int32, s.shape, 0)
    query = lax.broadcasted_iota(jnp.int32, s.shape, 1)
    return jnp.where(key <= query, s, -1e30)


def softmax_block(s, lo):
    s = s * EXP2_SCALE
    s = jnp.concatenate([s[:lo], causal(s[lo:])], axis=0) if lo else causal(s)
    raised = jnp.exp2(s - jnp.max(s, axis=0, keepdims=True))
    return raised * (1.0 / jnp.sum(raised, axis=0, keepdims=True))


def padded(block, tokens):
    missing = tokens - block.shape[0]
    return jnp.concatenate([block, jnp.zeros((missing, block.shape[1]), block.dtype)], axis=0) if missing else block


def forward_body(pick, gains, norm, out, mean, rstd):
    tokens, width = out.shape
    mean[...] = spread(norm[0])
    rstd[...] = spread(norm[1])

    def head(h):
        at = head_slice(h)
        x = pick(at).astype(F32)
        n = (x - mean[...]) * rstd[...]
        q = (n * gains[0:1, at]).astype(BF16)
        k = (n * gains[1:2, at]).astype(BF16)
        v = (n * gains[2:3, at]).astype(BF16)
        scores = dot(k, q, ((1,), (1,)))
        w = []
        for lo in range(0, tokens, BLOCK):
            hi = lo + BLOCK
            w.append(padded(softmax_block(scores[:hi, lo:hi], lo).astype(BF16), tokens))
        out[:, at] = (x + dot(jnp.concatenate(w, axis=1), v, ((0,), (0,)))).astype(BF16)

    each_head(width // HEAD_DIM, head)


def forward0_kernel(stream, gains, mine, other, out, rows, mean, rstd):
    norm = statistics_norm(mine, other, STREAM, out.shape[1])
    forward_body(lambda at: stream[:, at], gains, norm, out, mean, rstd)
    total, squares = moments(out[...].astype(F32))
    rows[...] = to_rows([None, None, total, squares])


def forward1_kernel(low, high, fresh, gains, late_mine, late_other, mine, other, out, mean, rstd):
    section = lax.axis_index("pipe")
    first = section == 0
    from_low = section <= lax.axis_size("pipe") // 2
    width = out.shape[1]
    norm = [
        jnp.where(first, a, b)
        for a, b in zip(statistics_norm(mine, other, FRESH, width), gradients_norm(late_mine, late_other, width))
    ]

    def pick(at):
        return jnp.where(first, fresh[:, at], jnp.where(from_low, low[:, at], high[:, at]))

    forward_body(pick, gains, norm, out, mean, rstd)


def local_call(kernel, out_shape, scratch, operands, name):
    return pl.pallas_call(
        kernel,
        in_specs=[VMEM] * len(operands),
        out_specs=[VMEM] * len(out_shape),
        out_shape=out_shape,
        scratch_shapes=scratch,
        compiler_params=PARAMS,
        name=name,
    )(*operands)


def forward(kernel, name, with_rows, *operands):
    tokens, width = operands[0].shape
    out_shape = [jax.ShapeDtypeStruct((tokens, width), BF16)]
    if with_rows:
        out_shape.append(jax.ShapeDtypeStruct((8, tokens), F32))
    return local_call(kernel, out_shape, [pltpu.VMEM((tokens, HEAD_DIM), F32)] * 2, operands, name)


def backward_body(pick, pick_gains, norm, before, dn_out, h_out, sums, mean, rstd, plain, cross):
    tokens, width = dn_out.shape
    mean[...] = spread(norm[0])
    rstd[...] = spread(norm[1])
    plain[...] = jnp.zeros_like(plain)
    cross[...] = jnp.zeros_like(cross)

    def head(h):
        at = head_slice(h)
        z, e = pick(h, at)
        n = (z.astype(F32) - mean[...]) * rstd[...]
        g = pick_gains(at)
        g0, g1, g2 = g[0:1], g[1:2], g[2:3]
        q = (n * g0).astype(BF16)
        k = (n * g1).astype(BF16)
        v = (n * g2).astype(BF16)
        scores = dot(k, q, ((1,), (1,)))
        dp = dot(v, e, ((1,), (1,)))
        w, ds = [], []
        for lo in range(0, tokens, BLOCK):
            hi = lo + BLOCK
            p = softmax_block(scores[:hi, lo:hi], lo)
            t = p * dp[:hi, lo:hi]
            w.append(padded(p.astype(BF16), tokens))
            ds.append(padded((t - p * jnp.sum(t, axis=0, keepdims=True)).astype(BF16), tokens))
        w, ds = jnp.concatenate(w, axis=1), jnp.concatenate(ds, axis=1)
        dv = dot(w, e, ((1,), (0,)))
        dk = dot(ds, q, ((1,), (0,)))
        dq = dot(ds, k, ((0,), (0,)))
        dn = dq * (g0 * SCALE) + dk * (g1 * SCALE) + dv * g2
        dn_out[:, at] = dn
        plain[...] += dn
        cross[...] += dn * n
        parts = [jnp.sum(grad * n, axis=0, keepdims=True) for grad in (dq, dk, dv)]
        total = jnp.concatenate([parts[0] * SCALE, parts[1] * SCALE, parts[2]], axis=0)
        h_out[0:3, at] = total if before is None else total + before(at)

    each_head(width // HEAD_DIM, head)
    sums[...] = to_rows([jnp.sum(plain[...], axis=-1, keepdims=True), jnp.sum(cross[...], axis=-1, keepdims=True)])


def finish_body(pick, norm, mine, other, dn, out, mean, rstd, plain, cross):
    means = (mine[0:2] + other[0:2]) * (1.0 / D)
    mean[...] = spread(norm[0])
    rstd[...] = spread(norm[1])
    plain[...] = spread(means[0:1])
    cross[...] = spread(means[1:2])

    def head(h):
        at = head_slice(h)
        z, e = pick(h, at)
        n = (z.astype(F32) - mean[...]) * rstd[...]
        out[:, at] = (e.astype(F32) + rstd[...] * (dn[:, at] - plain[...] - n * cross[...])).astype(BF16)

    each_head(out.shape[1] // HEAD_DIM, head)


def is_early():
    return lax.axis_index("pipe") < lax.axis_size("pipe") // 2


def pick_tick1(own_z, direct_z, around_z, own_e, got_e, loss_e):
    section, sections = lax.axis_index("pipe"), lax.axis_size("pipe")
    early = section < sections // 2
    here = section < sections // 2 - 1
    last = section == sections - 1

    def pick(h, at):
        first = jnp.minimum(h, DIRECT_HEADS - 1)
        second = jnp.maximum(h - DIRECT_HEADS, 0)
        got = jnp.where(h < DIRECT_HEADS, direct_z[:, head_slice(first)], around_z[:, head_slice(second)])
        e = jnp.where(last, loss_e[:, at], jnp.where(here, own_e[:, at], got_e[:, at]))
        return jnp.where(early, got, own_z[:, at]), e

    return pick


def late_backward0_kernel(z, e, gains, mine, other, *rest):
    @pl.when(jnp.logical_not(is_early()))
    def _():
        norm = statistics_norm(mine, other, OWN_STASH0, rest[0].shape[1])
        backward_body(lambda h, at: (z[:, at], e[:, at]), lambda at: gains[:, at], norm, None, *rest)


def early_backward0_kernel(z, e, gains, got_stats, dn, h_out, *rest):
    @pl.when(is_early())
    def _():
        tokens, width = dn.shape
        norm = normalizer(got_stats[0:1], got_stats[2:3])
        backward_body(lambda h, at: (z[:, at], e[:, at]), lambda at: gains[:, at], norm, None, dn, h_out, *rest)
        h_out[3:4, :] = jnp.zeros((1, width), F32)
        h_out[3:4, 0:tokens] = got_stats[1:2]
        h_out[3:4, tokens : 2 * tokens] = got_stats[3:4]


def late_finish0_kernel(z, e, stats_mine, stats_other, mine, other, dn, out, *rest):
    @pl.when(jnp.logical_not(is_early()))
    def _():
        norm = statistics_norm(stats_mine, stats_other, OWN_STASH0, out.shape[1])
        finish_body(lambda h, at: (z[:, at], e[:, at]), norm, mine, other, dn, out, *rest)


def early_finish0_kernel(z, e, got_stats, mine, other, dn, out, *rest):
    @pl.when(is_early())
    def _():
        norm = normalizer(got_stats[0:1], got_stats[2:3])
        finish_body(lambda h, at: (z[:, at], e[:, at]), norm, mine, other, dn, out, *rest)


def tick1_norm(mine, other, got_part, width):
    early, tokens = is_early(), mine.shape[1]
    sent = normalizer(got_part[3:4, 0:tokens], got_part[3:4, tokens : 2 * tokens])
    return [jnp.where(early, a, b) for a, b in zip(sent, statistics_norm(mine, other, OWN_STASH1, width))]


def backward1_kernel(oz, dz, az, oe, ge, le, gains, part, got_part, mine, other, dn, h_out, *rest):
    early = is_early()
    backward_body(
        pick_tick1(oz, dz, az, oe, ge, le),
        lambda at: gains[:, at],
        tick1_norm(mine, other, got_part, dn.shape[1]),
        lambda at: jnp.where(early, got_part[0:3, at], part[0:3, at]),
        dn,
        h_out,
        *rest,
    )


def finish1_kernel(oz, dz, az, oe, ge, le, stats_mine, stats_other, got_part, mine, other, dn, out, *rest):
    norm = tick1_norm(stats_mine, stats_other, got_part, out.shape[1])
    finish_body(pick_tick1(oz, dz, az, oe, ge, le), norm, mine, other, dn, out, *rest)


def backward(kernel, name, gain_rows, *operands):
    tokens, width = operands[0].shape
    out_shape = [
        jax.ShapeDtypeStruct((tokens, width), F32),
        jax.ShapeDtypeStruct((gain_rows, width), F32),
        jax.ShapeDtypeStruct((8, tokens), F32),
    ]
    return local_call(kernel, out_shape, [pltpu.VMEM((tokens, HEAD_DIM), F32)] * 4, operands, name)


def finish(kernel, name, *operands):
    tokens, width = operands[0].shape
    out_shape = [jax.ShapeDtypeStruct((tokens, width), BF16)]
    return local_call(kernel, out_shape, [pltpu.VMEM((tokens, HEAD_DIM), F32)] * 4, operands, name)[0]


def routes(sections):
    half, last = sections // 2, sections - 1
    to_next = [(s, s + 1) for s in range(last)]
    late_back = [(s, s - 1) for s in range(half, sections)]
    early_back = [(s, (s - 1) % half) for s in range(half)]
    early_on = [(s, (s + 1) % half) for s in range(half)]
    stash_ahead = [(last - s, (s - 1) % half) for s in range(half)]
    mirrored = [(last - s, s) for s in range(half)]
    across = [(last - s, s ^ 3) for s in range(half)]
    along = [(s ^ 3, s) for s in range(half)]
    return to_next, late_back, early_back, early_on, stash_ahead, mirrored, across, along


def over_tp(value, mask, sections=None):
    if sections is None:
        return lax.ppermute(value, "tp", [(i, i ^ mask) for i in range(PARTS)])
    pairs = [(s * PARTS + i, s * PARTS + (i ^ mask)) for s in sections for i in range(PARTS)]
    return lax.ppermute(value, ("pipe", "tp"), pairs)


def kept_statistics(both):
    return jnp.concatenate([both[KEPT_STASH0 : KEPT_STASH1 + 1], both[KEPT_STASH0 + 8 : KEPT_STASH1 + 9]])


def with_other_core(value, sections=None):
    return value + over_tp(value, 1, sections)


def per_device(
    stream_in, grad_in, fresh_batch, loss_grad, local_stash, partner_stash, norm_gains, stash_plan
):
    gains = norm_gains[0]
    cotangent = grad_in[0]
    width = fresh_batch.shape[1]
    to_next, late_back, early_back, early_on, stash_ahead, mirrored, across, along = routes(lax.axis_size("pipe"))

    def moved(value, pairs):
        return lax.ppermute(value, "pipe", pairs)

    def after(value, *others):
        return lax.optimization_barrier((value,) + others)[0]

    half = lax.axis_size("pipe") // 2
    low, high = range(half), range(half, 2 * half)
    sent0, direct, around, own_z0, own_z1, rows0 = pick(stash_plan, partner_stash, local_stash, stream_in, fresh_batch)
    stats_mine = join_statistics(rows0, over_tp(rows0, 1), width)
    late_other = over_tp(stats_mine, 2, high)
    low_other = over_tp(stats_mine, 2, low)
    late_stats = (stats_mine, late_other)
    stats = (stats_mine, late_other + low_other)
    kept_rows = kept_statistics(join_statistics(*late_stats, half_count(width)))
    got_gains = moved(gains, early_back)
    got_e0 = moved(cotangent, early_back)
    got_z0 = moved(after(sent0, stats_mine), stash_ahead)
    got_stats = moved(kept_rows, stash_ahead)
    crossed = moved(around, across)
    got_z1b = moved(crossed, along)
    late_grad, late_part, late_sums = backward(
        late_backward0_kernel, "late_backward0", 3, own_z0, cotangent, after(gains, got_gains, crossed), *late_stats
    )
    late_mine = with_other_core(late_sums)
    got_z1a = moved(after(direct, late_mine), mirrored)
    late_sums_other = over_tp(late_mine, 2, high)
    produced, out_rows = forward(
        forward0_kernel, "forward0", True, after(stream_in[0], late_mine), gains, *stats
    )
    got_out_rows = moved(out_rows, to_next)
    late_returned = finish(
        late_finish0_kernel, "late_finish0", own_z0, cotangent, *late_stats, late_mine, late_sums_other,
        after(late_grad, got_stats, produced)
    )
    came_back = moved(late_returned, late_back)
    early_grad, early_part, early_sums = backward(
        early_backward0_kernel, "early_backward0", 4, got_z0, got_e0, got_gains,
        after(got_stats, late_returned)
    )
    gain_back = moved(early_part, early_on)
    early_mine = with_other_core(early_sums)
    early_sums_other = over_tp(early_mine, 2, low)
    early_returned = finish(
        early_finish0_kernel, "early_finish0", got_z0, got_e0, got_stats, early_mine, early_sums_other,
        after(early_grad, gain_back)
    )
    arrived = moved(after(produced, early_returned, got_out_rows), to_next)
    tick1 = (own_z1, got_z1a, got_z1b, early_returned, came_back, loss_grad)
    last_grad, gain_total, last_sums = backward(
        backward1_kernel, "backward1", 3, *tick1, gains, late_part, gain_back, *late_stats
    )
    rows1 = last_sums + got_out_rows
    rows1_mine = join_gradients(rows1, over_tp(rows1, 1), width)
    sums1 = (rows1_mine, over_tp(rows1_mine, 2))
    fwd_out = forward(
        forward1_kernel, "forward1", False, arrived, arrived, fresh_batch, gains, *sums1, *stats
    )[0]
    bwd_out = finish(finish1_kernel, "finish1", *tick1, *late_stats, gain_back, *sums1, last_grad)
    return (fwd_out[None], bwd_out[None], gain_total[None])


def solution(mesh):
    placed = (
        P("pipe", None, "tp"),
        P("pipe", None, "tp"),
        P(None, "tp"),
        P(None, "tp"),
        P("pipe", None, None, "tp"),
        P("pipe", None, None, "tp"),
        P("pipe", None, "tp"),
        P(),
    )
    return jax.shard_map(
        per_device,
        mesh=mesh,
        in_specs=placed,
        out_specs=(P("pipe", None, "tp"), P("pipe", None, "tp"), P("pipe", None, "tp")),
        check_vma=False,
    )
```

```python
import jax
import jax.numpy as jnp
from jax import lax
from jax.experimental import pallas as pl
from jax.experimental.pallas import tpu as pltpu
from jax.sharding import PartitionSpec as P

HEAD_DIM = 128
BLOCK = 128
D = 6144
PARTS = 4
EPSILON = 1e-05
SCALE = HEAD_DIM ** (-0.5)
EXP2_SCALE = SCALE * 1.4426950408889634
HEADS_PER_STEP = 6
DIRECT_HEADS = 4
F32 = jnp.float32
BF16 = jnp.bfloat16
SMEM = pl.BlockSpec(memory_space=pltpu.SMEM)
VMEM = pl.BlockSpec(memory_space=pltpu.VMEM)
HBM = pl.BlockSpec(memory_space=pltpu.HBM)
PARAMS = pltpu.CompilerParams(vmem_limit_bytes=16 * 1024 * 1024)
ALL_VMEM = pltpu.CompilerParams(vmem_limit_bytes=56 * 1024 * 1024)


def dot(a, b, dims):
    return lax.dot_general(a, b, (dims, ((), ())), preferred_element_type=F32)


OWN_STASH0, OWN_STASH1, KEPT_STASH0, KEPT_STASH1, STREAM, FRESH = range(6)


def to_rows(columns):
    tokens = next(c for c in columns if c is not None).shape[0]
    lane = lax.broadcasted_iota(jnp.int32, (tokens, 128), 1)
    wide = jnp.zeros((tokens, 128), F32)
    for i, column in enumerate(columns):
        if column is not None:
            wide = jnp.where(lane == i, column, wide)
    return wide.T[: max(8, len(columns))]


def statistics_rows(found):
    columns = [None] * 16
    for place, (total, squares) in found.items():
        columns[place], columns[place + 8] = total, squares
    return to_rows(columns)


def spread(row):
    return jnp.broadcast_to(row, (HEAD_DIM, row.shape[1])).T


def moments(values):
    total = jnp.sum(values, axis=-1, keepdims=True)
    center = values - total * (1.0 / values.shape[-1])
    return total, jnp.sum(center * center, axis=-1, keepdims=True)


def joined_pair(sums, squares, other_sums, other_squares, count):
    apart = sums - other_sums
    return sums + other_sums, squares + other_squares + apart * apart * (0.5 / count)


def join_statistics(a, b, count):
    return jnp.concatenate(joined_pair(a[0:8], a[8:16], b[0:8], b[8:16], count), axis=0)


def join_gradients(a, b, count):
    total, squares = joined_pair(a[2:3], a[3:4], b[2:3], b[3:4], count)
    return jnp.concatenate([a[0:2] + b[0:2], total, squares, a[4:8]], axis=0)


def normalizer(total, squares):
    return total * (1.0 / D), lax.rsqrt(squares * (1.0 / D) + EPSILON)


def half_count(width):
    return width * (PARTS // 2)


def statistics_norm(mine, other, which, width):
    both = join_statistics(mine[...], other[...], half_count(width))
    return normalizer(both[which : which + 1], both[which + 8 : which + 9])


def gradients_norm(mine, other, width):
    both = join_gradients(mine[...], other[...], half_count(width))
    return normalizer(both[2:3], both[3:4])


def slot_of(plan, tick, section, first):
    return jnp.clip(plan[tick, section] - first, 0, 1)


def pick_kernel(plan, kept, own, stream, fresh, sent0, direct, around, own0, own1, rows, blocks, load_sems, store_sems):
    section, sections = lax.axis_index("pipe"), plan.shape[1]
    cut = direct.shape[1]
    partner = sections - 1 - section
    sources = [
        (KEPT_STASH1, kept.at[0, slot_of(plan, 1, partner, 2)]),
        (KEPT_STASH0, kept.at[0, slot_of(plan, 0, partner, 2)]),
        (OWN_STASH0, own.at[0, slot_of(plan, 0, section, 0)]),
        (OWN_STASH1, own.at[0, slot_of(plan, 1, section, 0)]),
        (STREAM, stream.at[0]),
        (FRESH, fresh),
    ]
    loads = [pltpu.make_async_copy(source, blocks.at[i], load_sems.at[i]) for i, (_, source) in enumerate(sources)]
    stores = [
        (0, pltpu.make_async_copy(blocks.at[0, :, pl.ds(0, cut)], direct, store_sems.at[0])),
        (0, pltpu.make_async_copy(blocks.at[0, :, pl.ds(cut, around.shape[1])], around, store_sems.at[1])),
        (1, pltpu.make_async_copy(blocks.at[1], sent0, store_sems.at[2])),
        (2, pltpu.make_async_copy(blocks.at[2], own0, store_sems.at[3])),
        (3, pltpu.make_async_copy(blocks.at[3], own1, store_sems.at[4])),
    ]
    for load in loads:
        load.start()
    found = {}
    for i, (place, _) in enumerate(sources):
        loads[i].wait()
        for block, store in stores:
            if block == i:
                store.start()
        found[place] = moments(blocks[i].astype(F32))
    rows[...] = statistics_rows(found)
    for _, store in stores:
        store.wait()


def pick(plan, kept, own, stream, fresh):
    tokens, width = fresh.shape
    cut = DIRECT_HEADS * HEAD_DIM
    whole = jax.ShapeDtypeStruct((tokens, width), BF16)
    return pl.pallas_call(
        pick_kernel,
        in_specs=[SMEM, HBM, HBM, HBM, HBM],
        out_specs=[HBM] * 5 + [VMEM],
        out_shape=[
            whole,
            jax.ShapeDtypeStruct((tokens, cut), BF16),
            jax.ShapeDtypeStruct((tokens, width - cut), BF16),
            whole,
            whole,
            jax.ShapeDtypeStruct((16, tokens), F32),
        ],
        scratch_shapes=[
            pltpu.VMEM((6, tokens, width), BF16),
            pltpu.SemaphoreType.DMA((6,)),
            pltpu.SemaphoreType.DMA((5,)),
        ],
        compiler_params=ALL_VMEM,
        name="pick",
    )(plan, kept, own, stream, fresh)


def head_slice(h):
    return pl.ds(pl.multiple_of(h * HEAD_DIM, HEAD_DIM), HEAD_DIM)


def each_head(heads, body):
    def step(i, carry):
        for j in range(HEADS_PER_STEP):
            body(i * HEADS_PER_STEP + j)
        return carry

    lax.fori_loop(0, heads // HEADS_PER_STEP, step, 0)


def causal(s):
    key = lax.broadcasted_iota(jnp.int32, s.shape, 0)
    query = lax.broadcasted_iota(jnp.int32, s.shape, 1)
    return jnp.where(key <= query, s, -1e30)


def softmax_block(s, lo):
    s = s * EXP2_SCALE
    s = jnp.concatenate([s[:lo], causal(s[lo:])], axis=0) if lo else causal(s)
    raised = jnp.exp2(s - jnp.max(s, axis=0, keepdims=True))
    return raised * (1.0 / jnp.sum(raised, axis=0, keepdims=True))


def padded(block, tokens):
    missing = tokens - block.shape[0]
    return jnp.concatenate([block, jnp.zeros((missing, block.shape[1]), block.dtype)], axis=0) if missing else block


def forward_body(pick, gains, norm, out, mean, rstd):
    tokens, width = out.shape
    mean[...] = spread(norm[0])
    rstd[...] = spread(norm[1])

    def head(h):
        at = head_slice(h)
        x = pick(at).astype(F32)
        n = (x - mean[...]) * rstd[...]
        q = (n * gains[0:1, at]).astype(BF16)
        k = (n * gains[1:2, at]).astype(BF16)
        v = (n * gains[2:3, at]).astype(BF16)
        scores = dot(k, q, ((1,), (1,)))
        w = []
        for lo in range(0, tokens, BLOCK):
            hi = lo + BLOCK
            w.append(padded(softmax_block(scores[:hi, lo:hi], lo).astype(BF16), tokens))
        out[:, at] = (x + dot(jnp.concatenate(w, axis=1), v, ((0,), (0,)))).astype(BF16)

    each_head(width // HEAD_DIM, head)


def forward0_kernel(stream, gains, mine, other, out, rows, mean, rstd):
    norm = statistics_norm(mine, other, STREAM, out.shape[1])
    forward_body(lambda at: stream[:, at], gains, norm, out, mean, rstd)
    total, squares = moments(out[...].astype(F32))
    rows[...] = to_rows([None, None, total, squares])


def forward1_kernel(arrived, fresh, gains, late_mine, late_other, mine, other, out, mean, rstd):
    first = lax.axis_index("pipe") == 0
    width = out.shape[1]
    norm = [
        jnp.where(first, a, b)
        for a, b in zip(statistics_norm(mine, other, FRESH, width), gradients_norm(late_mine, late_other, width))
    ]

    def pick(at):
        return jnp.where(first, fresh[:, at], arrived[:, at])

    forward_body(pick, gains, norm, out, mean, rstd)


def local_call(kernel, out_shape, scratch, operands, name):
    return pl.pallas_call(
        kernel,
        in_specs=[VMEM] * len(operands),
        out_specs=[VMEM] * len(out_shape),
        out_shape=out_shape,
        scratch_shapes=scratch,
        compiler_params=PARAMS,
        name=name,
    )(*operands)


def forward(kernel, name, with_rows, *operands):
    tokens, width = operands[0].shape
    out_shape = [jax.ShapeDtypeStruct((tokens, width), BF16)]
    if with_rows:
        out_shape.append(jax.ShapeDtypeStruct((8, tokens), F32))
    return local_call(kernel, out_shape, [pltpu.VMEM((tokens, HEAD_DIM), F32)] * 2, operands, name)


def backward_body(pick, pick_gains, norm, before, dn_out, h_out, sums, mean, rstd, plain, cross):
    tokens, width = dn_out.shape
    mean[...] = spread(norm[0])
    rstd[...] = spread(norm[1])
    plain[...] = jnp.zeros_like(plain)
    cross[...] = jnp.zeros_like(cross)

    def head(h):
        at = head_slice(h)
        z, e = pick(h, at)
        n = (z.astype(F32) - mean[...]) * rstd[...]
        g = pick_gains(at)
        g0, g1, g2 = g[0:1], g[1:2], g[2:3]
        q = (n * g0).astype(BF16)
        k = (n * g1).astype(BF16)
        v = (n * g2).astype(BF16)
        scores = dot(k, q, ((1,), (1,)))
        dp = dot(v, e, ((1,), (1,)))
        w, ds = [], []
        for lo in range(0, tokens, BLOCK):
            hi = lo + BLOCK
            p = softmax_block(scores[:hi, lo:hi], lo)
            t = p * dp[:hi, lo:hi]
            w.append(padded(p.astype(BF16), tokens))
            ds.append(padded((t - p * jnp.sum(t, axis=0, keepdims=True)).astype(BF16), tokens))
        w, ds = jnp.concatenate(w, axis=1), jnp.concatenate(ds, axis=1)
        dv = dot(w, e, ((1,), (0,)))
        dk = dot(ds, q, ((1,), (0,)))
        dq = dot(ds, k, ((0,), (0,)))
        dn = dq * (g0 * SCALE) + dk * (g1 * SCALE) + dv * g2
        dn_out[:, at] = dn
        plain[...] += dn
        cross[...] += dn * n
        parts = [jnp.sum(grad * n, axis=0, keepdims=True) for grad in (dq, dk, dv)]
        total = jnp.concatenate([parts[0] * SCALE, parts[1] * SCALE, parts[2]], axis=0)
        h_out[0:3, at] = total if before is None else total + before(at)

    each_head(width // HEAD_DIM, head)
    sums[...] = to_rows([jnp.sum(plain[...], axis=-1, keepdims=True), jnp.sum(cross[...], axis=-1, keepdims=True)])


def finish_body(pick, norm, mine, other, dn, out, mean, rstd, plain, cross):
    means = (mine[0:2] + other[0:2]) * (1.0 / D)
    mean[...] = spread(norm[0])
    rstd[...] = spread(norm[1])
    plain[...] = spread(means[0:1])
    cross[...] = spread(means[1:2])

    def head(h):
        at = head_slice(h)
        z, e = pick(h, at)
        n = (z.astype(F32) - mean[...]) * rstd[...]
        out[:, at] = (e.astype(F32) + rstd[...] * (dn[:, at] - plain[...] - n * cross[...])).astype(BF16)

    each_head(out.shape[1] // HEAD_DIM, head)


def is_early():
    return lax.axis_index("pipe") < lax.axis_size("pipe") // 2


def pick_tick1(own_z, direct_z, around_z, own_e, got_e, loss_e):
    section, sections = lax.axis_index("pipe"), lax.axis_size("pipe")
    early = section < sections // 2
    here = section < sections // 2 - 1
    last = section == sections - 1

    def pick(h, at):
        first = jnp.minimum(h, DIRECT_HEADS - 1)
        second = jnp.maximum(h - DIRECT_HEADS, 0)
        got = jnp.where(h < DIRECT_HEADS, direct_z[:, head_slice(first)], around_z[:, head_slice(second)])
        e = jnp.where(last, loss_e[:, at], jnp.where(here, own_e[:, at], got_e[:, at]))
        return jnp.where(early, got, own_z[:, at]), e

    return pick


def late_backward0_kernel(z, e, gains, mine, other, *rest):
    @pl.when(jnp.logical_not(is_early()))
    def _():
        norm = statistics_norm(mine, other, OWN_STASH0, rest[0].shape[1])
        backward_body(lambda h, at: (z[:, at], e[:, at]), lambda at: gains[:, at], norm, None, *rest)


def early_backward0_kernel(z, e, gains, got_stats, dn, h_out, *rest):
    @pl.when(is_early())
    def _():
        tokens, width = dn.shape
        norm = normalizer(got_stats[0:1], got_stats[2:3])
        backward_body(lambda h, at: (z[:, at], e[:, at]), lambda at: gains[:, at], norm, None, dn, h_out, *rest)
        h_out[3:4, :] = jnp.zeros((1, width), F32)
        h_out[3:4, 0:tokens] = got_stats[1:2]
        h_out[3:4, tokens : 2 * tokens] = got_stats[3:4]


def late_finish0_kernel(z, e, stats_mine, stats_other, mine, other, dn, out, *rest):
    @pl.when(jnp.logical_not(is_early()))
    def _():
        norm = statistics_norm(stats_mine, stats_other, OWN_STASH0, out.shape[1])
        finish_body(lambda h, at: (z[:, at], e[:, at]), norm, mine, other, dn, out, *rest)


def early_finish0_kernel(z, e, got_stats, mine, other, dn, out, *rest):
    @pl.when(is_early())
    def _():
        norm = normalizer(got_stats[0:1], got_stats[2:3])
        finish_body(lambda h, at: (z[:, at], e[:, at]), norm, mine, other, dn, out, *rest)


def tick1_norm(mine, other, got_part, width):
    early, tokens = is_early(), mine.shape[1]
    sent = normalizer(got_part[3:4, 0:tokens], got_part[3:4, tokens : 2 * tokens])
    return [jnp.where(early, a, b) for a, b in zip(sent, statistics_norm(mine, other, OWN_STASH1, width))]


def backward1_kernel(oz, dz, az, oe, ge, le, gains, part, got_part, mine, other, dn, h_out, *rest):
    early = is_early()
    backward_body(
        pick_tick1(oz, dz, az, oe, ge, le),
        lambda at: gains[:, at],
        tick1_norm(mine, other, got_part, dn.shape[1]),
        lambda at: jnp.where(early, got_part[0:3, at], part[0:3, at]),
        dn,
        h_out,
        *rest,
    )


def finish1_kernel(oz, dz, az, oe, ge, le, stats_mine, stats_other, got_part, mine, other, dn, out, *rest):
    norm = tick1_norm(stats_mine, stats_other, got_part, out.shape[1])
    finish_body(pick_tick1(oz, dz, az, oe, ge, le), norm, mine, other, dn, out, *rest)


def backward(kernel, name, gain_rows, *operands):
    tokens, width = operands[0].shape
    out_shape = [
        jax.ShapeDtypeStruct((tokens, width), F32),
        jax.ShapeDtypeStruct((gain_rows, width), F32),
        jax.ShapeDtypeStruct((8, tokens), F32),
    ]
    return local_call(kernel, out_shape, [pltpu.VMEM((tokens, HEAD_DIM), F32)] * 4, operands, name)


def finish(kernel, name, *operands):
    tokens, width = operands[0].shape
    out_shape = [jax.ShapeDtypeStruct((tokens, width), BF16)]
    return local_call(kernel, out_shape, [pltpu.VMEM((tokens, HEAD_DIM), F32)] * 4, operands, name)[0]


def routes(sections):
    half, last = sections // 2, sections - 1
    to_next = [(s, s + 1) for s in range(last)]
    late_back = [(s, s - 1) for s in range(half, sections)]
    early_back = [(s, (s - 1) % half) for s in range(half)]
    early_on = [(s, (s + 1) % half) for s in range(half)]
    stash_ahead = [(last - s, (s - 1) % half) for s in range(half)]
    mirrored = [(last - s, s) for s in range(half)]
    across = [(last - s, s ^ 3) for s in range(half)]
    along = [(s ^ 3, s) for s in range(half)]
    return to_next, late_back, early_back, early_on, stash_ahead, mirrored, across, along


def over_tp(value, mask, sections=None):
    if sections is None:
        return lax.ppermute(value, "tp", [(i, i ^ mask) for i in range(PARTS)])
    pairs = [(s * PARTS + i, s * PARTS + (i ^ mask)) for s in sections for i in range(PARTS)]
    return lax.ppermute(value, ("pipe", "tp"), pairs)


def kept_statistics(both):
    return jnp.concatenate([both[KEPT_STASH0 : KEPT_STASH1 + 1], both[KEPT_STASH0 + 8 : KEPT_STASH1 + 9]])


def with_other_core(value, sections=None):
    return value + over_tp(value, 1, sections)


def per_device(
    stream_in, grad_in, fresh_batch, loss_grad, local_stash, partner_stash, norm_gains, stash_plan
):
    gains = norm_gains[0]
    cotangent = grad_in[0]
    width = fresh_batch.shape[1]
    to_next, late_back, early_back, early_on, stash_ahead, mirrored, across, along = routes(lax.axis_size("pipe"))

    def moved(value, pairs):
        return lax.ppermute(value, "pipe", pairs)

    def after(value, *others):
        return lax.optimization_barrier((value,) + others)[0]

    half = lax.axis_size("pipe") // 2
    low, high = range(half), range(half, 2 * half)
    sent0, direct, around, own_z0, own_z1, rows0 = pick(stash_plan, partner_stash, local_stash, stream_in, fresh_batch)
    stats_mine = join_statistics(rows0, over_tp(rows0, 1), width)
    late_other = over_tp(stats_mine, 2, high)
    low_other = over_tp(stats_mine, 2, low)
    late_stats = (stats_mine, late_other)
    stats = (stats_mine, late_other + low_other)
    kept_rows = kept_statistics(join_statistics(*late_stats, half_count(width)))
    got_gains = moved(gains, early_back)
    got_e0 = moved(cotangent, early_back)
    got_z0 = moved(after(sent0, stats_mine), stash_ahead)
    got_stats = moved(kept_rows, stash_ahead)
    crossed = moved(around, across)
    got_z1b = moved(crossed, along)
    late_grad, late_part, late_sums = backward(
        late_backward0_kernel, "late_backward0", 3, own_z0, cotangent, after(gains, got_gains, crossed), *late_stats
    )
    late_mine = with_other_core(late_sums)
    got_z1a = moved(after(direct, late_mine), mirrored)
    late_sums_other = over_tp(late_mine, 2, high)
    produced, out_rows = forward(
        forward0_kernel, "forward0", True, after(stream_in[0], late_mine), gains, *stats
    )
    got_out_rows = moved(out_rows, to_next)
    late_returned = finish(
        late_finish0_kernel, "late_finish0", own_z0, cotangent, *late_stats, late_mine, late_sums_other,
        after(late_grad, got_stats, produced)
    )
    came_back = moved(late_returned, late_back)
    early_grad, early_part, early_sums = backward(
        early_backward0_kernel, "early_backward0", 4, got_z0, got_e0, got_gains,
        after(got_stats, late_returned)
    )
    gain_back = moved(early_part, early_on)
    early_mine = with_other_core(early_sums)
    early_sums_other = over_tp(early_mine, 2, low)
    early_returned = finish(
        early_finish0_kernel, "early_finish0", got_z0, got_e0, got_stats, early_mine, early_sums_other,
        after(early_grad, gain_back)
    )
    arrived = moved(after(produced, early_returned, got_out_rows), to_next)
    tick1 = (own_z1, got_z1a, got_z1b, early_returned, came_back, loss_grad)
    last_grad, gain_total, last_sums = backward(
        backward1_kernel, "backward1", 3, *tick1, gains, late_part, gain_back, *late_stats
    )
    rows1 = last_sums + got_out_rows
    rows1_mine = join_gradients(rows1, over_tp(rows1, 1), width)
    sums1 = (rows1_mine, over_tp(rows1_mine, 2))
    fwd_out = forward(
        forward1_kernel, "forward1", False, arrived, fresh_batch, gains, *sums1, *stats
    )[0]
    bwd_out = finish(finish1_kernel, "finish1", *tick1, *late_stats, gain_back, *sums1, last_grad)
    return (fwd_out[None], bwd_out[None], gain_total[None])


def solution(mesh):
    placed = (
        P("pipe", None, "tp"),
        P("pipe", None, "tp"),
        P(None, "tp"),
        P(None, "tp"),
        P("pipe", None, None, "tp"),
        P("pipe", None, None, "tp"),
        P("pipe", None, "tp"),
        P(),
    )
    return jax.shard_map(
        per_device,
        mesh=mesh,
        in_specs=placed,
        out_specs=(P("pipe", None, "tp"), P("pipe", None, "tp"), P("pipe", None, "tp")),
        check_vma=False,
    )
```
